32 devices in a mesh: groups: 2 (over x), dp: 16 (over z, y, core).
Axes of the slice: x: 2, y: 2, z: 4, core: 2. Of those that a mesh axis runs over, the one named last changes fastest.
Arguments:
- hidden: bfloat16 [4096, 28672], P('groups', 'dp'), parts along dimension 0, may hold values from -6 to 6
- grad_out: bfloat16 [4096, 8192], P('groups', 'dp'), parts along dimension 0, may hold values from -0.1875 to 0.1875
- in_factor: bfloat16 [28672, 64], P('dp'), may hold values from -0.03125 to 0.03125
- out_factor: bfloat16 [8192, 64], P('dp'), may hold values from -0.0625 to 0.0625
- queries: bfloat16 [512, 4096], P('dp'), may hold values from -0.09375 to 0.09375
Outputs:
- logged: float32 [2, 4096], P('groups', 'dp'), parts along dimension 0
- scores: float32 [2, 512], P('groups', 'dp'), parts along dimension 0
The draws below stay inside these ranges and needn't reach their ends.
There are 2 independent parts, one for each index of `groups`. The reference program is written for one: setup_inputs(seed, part) draws one part's arguments, and reference() takes and returns one part's arrays. A program takes and returns all parts, laid end to end along the dimension named above; an argument that names none is the same for every part. Nothing has to cross between parts.
All inputs are finite; a program needn't handle non-finite values.
Results may differ from the reference program's by a relative error of at most 0.0041.
Values may be sent and summed in bfloat16 or wider, within the bound.
A program may use at most 64 MiB of HBM per device.

```python
import jax
import jax.numpy as jnp
from jax import lax

D = 8192
FF = 28672
RIN = 64
ROUT = 64
NQ = 512
SEQS = 1
TOKENS = 2048
SEQ_LEN = 2048
FEATURES = 4096


def spiked(result, own_key, source, target, blocks, factor):
    owner, partner = [(jnp.arange(result.shape[dim]) // (result.shape[dim] // blocks)).reshape([-1 if axis == dim else 1 for axis in range(result.ndim)]) for dim in (source, target)]
    chosen = jax.random.permutation(own_key, blocks)[partner]
    strong = (owner == chosen) | (owner == (partner + blocks // 2) % blocks)
    return jnp.where(strong, factor * result, result)


def levels(rng, shape, pieces, low, largest):
    gain = 1.0
    for axis_at, parts in pieces:
        heights = jax.random.uniform(jax.random.fold_in(jax.random.fold_in(rng, 6), axis_at), (parts,), jnp.float32, low / len(pieces), largest / len(pieces))
        gain = gain * jnp.repeat(jnp.exp(heights), shape[axis_at] // parts).reshape((-1,) + (1,) * (len(shape) - 1 - axis_at))
    return gain


def noise(rng, shape, spread, bound, cuts=(), kind=jnp.bfloat16):
    array = spread * jax.random.normal(rng, shape, jnp.float32)
    if cuts:
        array = array * levels(rng, shape, cuts, -0.22, 0.18)
    return jnp.clip(array, -bound, bound).astype(kind)


def heavy_noise(own_key, shape, spread, bound, shards, heavy, dtype=jnp.bfloat16):
    values = spread * jax.random.normal(own_key, shape, jnp.float32)
    if shards:
        values = values * levels(own_key, shape, shards, -0.22, 0.18)
    return jnp.clip(spiked(values, jax.random.fold_in(own_key, 3), *heavy), -bound, bound).astype(dtype)


def setup_inputs(seed: int = 0, part: int = 0) -> dict:
    streams_of = jax.random.split(jax.random.key(seed), 6)
    part_splits = jax.random.split(jax.random.fold_in(streams_of[5], part), 6)
    return {
        "hidden": heavy_noise(part_splits[0], (TOKENS, FF), 1.0, 6.0, ((1, 16),), (1, 0, 16, 2.0)),
        "grad_out": heavy_noise(part_splits[1], (TOKENS, D), SEQ_LEN ** -0.5, 0.1875, ((1, 16),), (1, 0, 16, 2.0)),
        "in_factor": noise(streams_of[2], (FF, RIN), FF ** -0.5, 0.03125, ((0, 16),)),
        "out_factor": noise(streams_of[3], (D, ROUT), D ** -0.5, 0.0625, ((0, 16),)),
        "queries": noise(streams_of[4], (NQ, FEATURES), FEATURES ** -0.5, 0.09375, ((0, 16),)),
    }


def reference(hidden, grad_out, in_factor, out_factor, queries):
    in_proj = jnp.dot(hidden, in_factor, preferred_element_type=jnp.float32).astype(jnp.bfloat16)
    out_proj = jnp.dot(grad_out, out_factor, preferred_element_type=jnp.float32).astype(jnp.bfloat16)
    in_seq = in_proj.reshape(SEQS, SEQ_LEN, RIN).astype(jnp.float32)
    out_seq = out_proj.reshape(SEQS, SEQ_LEN, ROUT).astype(jnp.float32)
    logged = jnp.einsum("sti,stj->sij", in_seq, out_seq, precision=lax.Precision.HIGHEST)
    logged = logged.reshape(SEQS, RIN * ROUT)
    scores = jnp.dot(logged, queries.astype(jnp.float32).T, precision=lax.Precision.HIGHEST)
    return logged, scores
```

```python
import functools

import jax
import jax.numpy as jnp
from jax import lax
from jax.experimental import pallas as pl
from jax.experimental.pallas import tpu as pltpu
from jax.sharding import PartitionSpec as P

CORES = 2
LANES = 128
VMEM_BYTES = 56 * 2**20


def each(count, body):
    if count <= 16:
        for step in range(count):
            body(step)
    else:
        pl.loop(0, count)(body)


def kernel(
    n, inner, outer, owners,
    hidden, grad, a_in, b_in, queries,
    logged, scores,
    hbuf, gbuf, a_buf, b_buf, q_buf, wa, wb,
    part_send, part_recv, own, y_send, y_recv, z_send, z_recv, total,
    l_send, l_recv, l_own, l_all,
    in_sem, cs_sem, cr_sem, ys_sem, yr_sem, zs_sem, zr_sem, ls_sem, lr_sem, gs_sem, gr_sem,
):
    me = lax.axis_index("dp")
    core = lax.rem(me, CORES)
    chip = me // CORES
    mid = lax.rem(chip, inner)
    out = chip // inner
    chunk = hbuf.shape[1]
    block = chunk // inner
    rank = a_in.shape[1]
    rows = l_own.shape[0]

    def remote(src, dst, send, recv, target):
        return pltpu.make_async_remote_copy(
            src_ref=src, dst_ref=dst, send_sem=send, recv_sem=recv,
            device_id={"dp": target}, device_id_type=pl.DeviceIdType.MESH,
        )

    def inputs(step, mine):
        half = core if mine else 1 - core
        first = (half * outer + lax.rem(out + 1 + step, outer)) * chunk
        span = pl.ds(pl.multiple_of(first, chunk), chunk)
        slot = 2 * step + mine
        return (
            pltpu.make_async_copy(hidden.at[span], hbuf.at[slot], in_sem.at[2 * slot]),
            pltpu.make_async_copy(grad.at[span], gbuf.at[slot], in_sem.at[2 * slot + 1]),
        )

    last = 4 * outer
    copy_a = pltpu.make_async_copy(a_in, a_buf, in_sem.at[last])
    copy_b = pltpu.make_async_copy(b_in, b_buf, in_sem.at[last + 1])
    copy_q = pltpu.make_async_copy(queries, q_buf, in_sem.at[last + 2])
    copy_a.start()
    copy_b.start()
    order = [(0, 0)]
    for step in range(1, outer):
        order += [(step, 0), (step - 1, 1)]
    order += [(outer - 1, 1)]
    for step, mine in order:
        for copy in inputs(step, mine):
            copy.start()
    copy_q.start()

    barrier = pltpu.get_barrier_semaphore()

    def greet(d):
        pl.semaphore_signal(
            barrier, inc=1, device_id={"dp": lax.rem(me + 1 + d, n)},
            device_id_type=pl.DeviceIdType.MESH,
        )

    each(n - 1, greet)

    row = lax.broadcasted_iota(jnp.int32, (rank, 2 * rank), 0)
    lane = lax.broadcasted_iota(jnp.int32, (rank, 2 * rank), 1)
    half = rank // 2
    source = jnp.where(lane < half, 2 * lane, 2 * (lane - half) + 1)
    take_a = jnp.where((lane < rank) & (row == source), 1.0, 0.0).astype(jnp.bfloat16)
    take_b = jnp.where(lane - rank == row, 1.0, 0.0).astype(jnp.bfloat16)
    copy_a.wait()
    wa[...] = jnp.dot(a_buf[...], take_a, preferred_element_type=jnp.float32).astype(jnp.bfloat16)
    copy_b.wait()
    wb[...] = jnp.dot(b_buf[...], take_b, preferred_element_type=jnp.float32).astype(jnp.bfloat16)

    def project(step, mine):
        for copy in inputs(step, mine):
            copy.wait()
        slot = 2 * step + mine
        return jnp.dot(
            hbuf[slot], wa[...], preferred_element_type=jnp.float32
        ) + jnp.dot(gbuf[slot], wb[...], preferred_element_type=jnp.float32)

    def to_core(step):
        return remote(part_send.at[step], part_recv.at[step], cs_sem.at[step], cr_sem.at[step], 1 - core + chip * CORES)

    def to_mid(step, d):
        index = step * max(inner - 1, 1) + d
        target = (out * inner + lax.rem(mid + 1 + d, inner)) * CORES + core
        return remote(y_send.at[index], y_recv.at[index], ys_sem.at[index], yr_sem.at[index], target)

    def to_out(step):
        target = (lax.rem(out + 1 + step, outer) * inner + mid) * CORES + core
        return remote(z_send.at[step], z_recv.at[step], zs_sem.at[step], zr_sem.at[step], target)

    def chip_sum(step, place):
        span = pl.ds(pl.multiple_of(place * block, block), block)
        return own[step, span, :] + part_recv[step, span, :]

    def stage_a(step):
        part_send[step] = project(step, 0)
        if step == 0:
            pl.semaphore_wait(barrier, n - 1)
        to_core(step).start()

    def stage_b(step):
        own[step] = project(step, 1)

    def stage_c(step):
        to_core(step).wait_recv()
        for d in range(inner - 1):
            y_send[step * (inner - 1) + d] = chip_sum(step, lax.rem(mid + 1 + d, inner)).astype(jnp.bfloat16)
            to_mid(step, d).start()

    def stage_d(step):
        value = chip_sum(step, mid)
        for d in range(inner - 1):
            to_mid(step, d).wait_recv()
            value = value + y_recv[step * (inner - 1) + d].astype(jnp.float32)
        if step < outer - 1:
            z_send[step] = value.astype(jnp.bfloat16)
            to_out(step).start()
        else:
            total[...] = value

    stage_a(0)
    for step in range(1, outer):
        stage_a(step)
        stage_b(step - 1)
        stage_c(step - 1)
        if step >= 2:
            stage_d(step - 2)
    stage_b(outer - 1)
    stage_c(outer - 1)
    if outer >= 2:
        stage_d(outer - 2)
    stage_d(outer - 1)

    value = total[...]
    for step in range(outer - 1):
        to_out(step).wait_recv()
        value = value + z_recv[step].astype(jnp.float32)
    gram = lax.dot_general(
        value, value, (((0,), (0,)), ((), ())),
        precision=lax.Precision.HIGHEST, preferred_element_type=jnp.float32,
    )
    flat = jnp.concatenate([gram[:half, rank:], gram[half:rank, rank:]], axis=1)
    for e in range(owners):
        l_send[e] = flat[e * rows:(e + 1) * rows, :]

    def guard(condition, body):
        if owners == n:
            body()
        else:
            pl.when(condition)(body)

    def to_owner(d):
        target = lax.rem(me + 1 + d, n)
        slot = target if owners == n else jnp.minimum(target, owners - 1)
        return target, remote(l_send.at[slot], l_recv.at[d], ls_sem, lr_sem, target)

    def send_owner(d):
        target, copy = to_owner(d)
        guard(target < owners, copy.start)

    each(n - 1, send_owner)

    def to_all(d):
        target = lax.rem(me + 1 + d, n)
        return remote(l_own, l_all.at[me if owners == n else jnp.minimum(me, owners - 1)], gs_sem, gr_sem, target)

    def reduce_and_share():
        pltpu.make_async_copy(l_recv, l_recv, lr_sem).wait()
        result = l_send[me if owners == n else jnp.minimum(me, owners - 1)]
        for d in range(n - 1):
            result = result + l_recv[d]
        l_own[...] = result
        each(n - 1, lambda d: to_all(d).start())
        l_all[me if owners == n else jnp.minimum(me, owners - 1)] = result

    guard(me < owners, reduce_and_share)

    def sent(count, ref, sem):
        if count:
            view = ref.at[pl.ds(0, count)]
            pltpu.make_async_copy(view, view, sem).wait()

    def wait_others():
        sent(owners - 1, l_send, ls_sem)
        for step in range(outer):
            to_core(step).wait_send()
            for d in range(inner - 1):
                to_mid(step, d).wait_send()
        for step in range(outer - 1):
            to_out(step).wait_send()

    if owners == n:
        wait_others()
    else:
        for step in range(outer):
            to_core(step).wait_send()
            for d in range(inner - 1):
                to_mid(step, d).wait_send()
        for step in range(outer - 1):
            to_out(step).wait_send()
        pl.when(me < owners)(lambda: sent(owners - 1, l_send, ls_sem))
        pl.when(me >= owners)(lambda: sent(owners, l_send, ls_sem))
    copy_q.wait()

    if owners == n:
        sent(n - 1, l_all, gr_sem)
    else:
        pl.when(me < owners)(lambda: sent(owners - 1, l_all, gr_sem))
        pl.when(me >= owners)(lambda: sent(owners, l_all, gr_sem))

    acc = jnp.zeros((queries.shape[0], LANES), jnp.float32)
    for e in range(owners):
        for r in range(rows):
            first = (e * rows + r) * LANES
            acc = acc + q_buf[:, first:first + LANES].astype(jnp.float32) * l_all[e, r:r + 1, :]
    dots = jnp.sum(acc, axis=1, keepdims=True)
    row = lax.broadcasted_iota(jnp.int32, acc.shape, 0)
    lane = lax.broadcasted_iota(jnp.int32, acc.shape, 1)
    across = jnp.sum(jnp.where(row == lane, dots, 0.0), axis=0, keepdims=True)
    scores[...] = across[:, :scores.shape[1]]
    if logged.shape[0] == rows:
        logged[...] = l_own[...]
    else:
        for e in range(owners):
            logged[e * rows:(e + 1) * rows, :] = l_all[e]

    def shared():
        pltpu.make_async_copy(l_recv, l_recv, gs_sem).wait()

    guard(me < owners, shared)


def on_device(hidden, grad, in_factor, out_factor, queries):
    n = lax.axis_size("dp")
    tokens, width_h = hidden.shape
    width_g = grad.shape[1]
    rank = in_factor.shape[1]
    features = queries.shape[1]
    chips = n // CORES
    inner = 2 ** ((chips.bit_length() - 1) // 2)
    outer = chips // inner
    block = tokens // n
    chunk = block * inner
    flat_rows = features // LANES
    owners = min(n, flat_rows)
    rows = flat_rows // owners
    share = features // n
    whole_rows = share % LANES == 0
    f32, b16 = jnp.float32, jnp.bfloat16
    dma = pltpu.SemaphoreType.DMA
    mids = max(outer * (inner - 1), 1)
    outs = max(outer - 1, 1)
    flops = 2 * tokens * (width_h + width_g) * 2 * rank
    logged, scores = pl.pallas_call(
        functools.partial(kernel, n, inner, outer, owners),
        out_shape=(
            jax.ShapeDtypeStruct((rows if whole_rows else flat_rows, LANES), f32),
            jax.ShapeDtypeStruct((1, queries.shape[0]), f32),
        ),
        in_specs=[pl.BlockSpec(memory_space=pl.ANY)] * 5,
        out_specs=(pl.BlockSpec(memory_space=pltpu.VMEM),) * 2,
        scratch_shapes=[
            pltpu.VMEM((2 * outer, chunk, width_h), b16),
            pltpu.VMEM((2 * outer, chunk, width_g), b16),
            pltpu.VMEM(in_factor.shape, b16),
            pltpu.VMEM(out_factor.shape, b16),
            pltpu.VMEM(queries.shape, b16),
            pltpu.VMEM((width_h, 2 * rank), b16),
            pltpu.VMEM((width_g, 2 * rank), b16),
            pltpu.VMEM((outer, chunk, 2 * rank), f32),
            pltpu.VMEM((outer, chunk, 2 * rank), f32),
            pltpu.VMEM((outer, chunk, 2 * rank), f32),
            pltpu.VMEM((mids, block, 2 * rank), b16),
            pltpu.VMEM((mids, block, 2 * rank), b16),
            pltpu.VMEM((outs, block, 2 * rank), b16),
            pltpu.VMEM((outs, block, 2 * rank), b16),
            pltpu.VMEM((block, 2 * rank), f32),
            pltpu.VMEM((owners, rows, LANES), f32),
            pltpu.VMEM((n - 1, rows, LANES), f32),
            pltpu.VMEM((rows, LANES), f32),
            pltpu.VMEM((owners, rows, LANES), f32),
            dma((4 * outer + 3,)),
            dma((outer,)),
            dma((outer,)),
            dma((mids,)),
            dma((mids,)),
            dma((outs,)),
            dma((outs,)),
            dma,
            dma,
            dma,
            dma,
        ],
        compiler_params=pltpu.CompilerParams(
            collective_id=0, has_side_effects=True, vmem_limit_bytes=VMEM_BYTES
        ),
        cost_estimate=pl.CostEstimate(
            flops=flops, bytes_accessed=2 * tokens * (width_h + width_g), transcendentals=0
        ),
    )(hidden, grad, in_factor, out_factor, queries)
    if whole_rows:
        return logged.reshape(1, share), scores
    flat = logged.reshape(1, features)
    return lax.dynamic_slice_in_dim(flat, lax.axis_index("dp") * share, share, 1), scores


def solution(mesh):
    in_specs = (P("groups", "dp"), P("groups", "dp"), P("dp", None), P("dp", None), P("dp", None))
    out_specs = (P("groups", "dp"), P("groups", "dp"))
    return jax.shard_map(
        on_device, mesh=mesh, in_specs=in_specs, out_specs=out_specs, check_vma=False
    )
```

```python
import functools

import jax
import jax.numpy as jnp
from jax import lax
from jax.experimental import pallas as pl
from jax.experimental.pallas import tpu as pltpu
from jax.sharding import PartitionSpec as P

CORES = 2
PAIR = 2
CHUNKS = 4
LANES = 128
VMEM_BYTES = 56 * 2**20


def flip(value, mask):
    bit = 1
    while bit <= mask:
        if mask & bit:
            value = value + bit - 2 * bit * lax.rem(value // bit, 2)
        bit *= 2
    return value


def kernel(
    n,
    hidden, grad, a_in, b_in, queries,
    result,
    hbuf, gbuf, a_buf, b_buf, q_buf, wa, wb,
    part_send, part_recv, own, z_send, z_recv,
    l_part, l_recv, l_half, h_recv, l_all,
    in_sem, cs_sem, cr_sem, zs_sem, zr_sem,
    ps_sem, pr_sem, hs_sem, hr_sem, as_sem, ar_sem,
):
    me = lax.axis_index("dp")
    core = lax.rem(me, CORES)
    chip = me // CORES
    chips = n // CORES
    chunk = hbuf.shape[1]
    block = own.shape[0] // chips
    rank = a_in.shape[0]
    half_rows = l_half.shape[0]
    partner = chip * CORES + 1 - core

    def remote(src, dst, send, recv, target):
        return pltpu.make_async_remote_copy(
            src_ref=src, dst_ref=dst, send_sem=send, recv_sem=recv,
            device_id={"dp": target}, device_id_type=pl.DeviceIdType.MESH,
        )

    barrier = pltpu.get_barrier_semaphore()

    def greet(target):
        pl.semaphore_signal(
            barrier, inc=1, device_id={"dp": target}, device_id_type=pl.DeviceIdType.MESH
        )

    for mask in range(chips - 1, 0, -1):
        greet(flip(chip, mask) * CORES + core)
    greet(partner)

    def inputs(mine, step):
        first = ((core if mine else 1 - core) * CHUNKS + step) * chunk
        span = pl.ds(pl.multiple_of(first, chunk), chunk)
        slot = mine * CHUNKS + step
        return (
            pltpu.make_async_copy(hidden.at[span], hbuf.at[slot], in_sem.at[2 * slot]),
            pltpu.make_async_copy(grad.at[span], gbuf.at[slot], in_sem.at[2 * slot + 1]),
        )

    last = 4 * CHUNKS
    copy_a = pltpu.make_async_copy(a_in, a_buf, in_sem.at[last])
    copy_b = pltpu.make_async_copy(b_in, b_buf, in_sem.at[last + 1])
    width_q = q_buf.shape[2]
    copy_q = [
        pltpu.make_async_copy(
            queries.at[:, pl.ds(side * width_q, width_q)], q_buf.at[side], in_sem.at[last + 2 + side]
        )
        for side in range(CORES)
    ]
    copy_a.start()
    copy_b.start()
    order = [(mine, step) for mine in range(2) for step in range(CHUNKS)]
    for mine, step in order:
        for copy in inputs(mine, step):
            copy.start()
    for copy in copy_q:
        copy.start()

    row = lax.broadcasted_iota(jnp.int32, (rank, 2 * rank), 0)
    lane = lax.broadcasted_iota(jnp.int32, (rank, 2 * rank), 1)
    half = rank // 2
    source = jnp.where(lane < half, 2 * lane, 2 * (lane - half) + 1)
    take_a = jnp.where((lane < rank) & (row == source), 1.0, 0.0).astype(jnp.bfloat16)
    take_b = jnp.where(lane - rank == row, 1.0, 0.0).astype(jnp.bfloat16)

    def spread(factor, take):
        return lax.dot_general(
            factor[...], take, (((0,), (0,)), ((), ())), preferred_element_type=jnp.float32
        ).astype(jnp.bfloat16)

    copy_a.wait()
    wa[...] = spread(a_buf, take_a)
    copy_b.wait()
    wb[...] = spread(b_buf, take_b)

    for mine, step in order:
        for copy in inputs(mine, step):
            copy.wait()
        slot = mine * CHUNKS + step
        span = pl.ds(step * chunk, chunk)
        (own if mine else part_send)[span, :] = jnp.dot(
            hbuf[slot], wa[...], preferred_element_type=jnp.float32
        ) + jnp.dot(gbuf[slot], wb[...], preferred_element_type=jnp.float32)

    pl.semaphore_wait(barrier, chips)

    def to_core(piece):
        first = flip(chip // PAIR, piece) * (PAIR * block)
        span = pl.ds(pl.multiple_of(first, PAIR * block), PAIR * block)
        return remote(part_send.at[span], part_recv.at[span], cs_sem.at[piece], cr_sem.at[piece], partner)

    def to_chip(mask):
        slot = mask - 1
        target = flip(chip, mask) * CORES + core
        return remote(z_send.at[slot], z_recv.at[slot], zs_sem.at[slot], zr_sem.at[slot], target)

    def chip_sum(mask):
        span = pl.ds(pl.multiple_of(flip(chip, mask) * block, block), block)
        return own[span, :] + part_recv[span, :]

    pieces = range(chips // PAIR - 1, -1, -1)
    for piece in pieces:
        to_core(piece).start()
    for piece in pieces:
        to_core(piece).wait_recv()
        for mask in (2 * piece + 1, 2 * piece):
            if mask:
                z_send[mask - 1] = chip_sum(mask).astype(jnp.bfloat16)
                to_chip(mask).start()
    value = chip_sum(0)
    for mask in range(1, chips):
        to_chip(mask).wait_recv()
        value = value + z_recv[mask - 1].astype(jnp.float32)

    gram = lax.dot_general(
        value, value, (((0,), (0,)), ((), ())),
        precision=lax.Precision.HIGHEST, preferred_element_type=jnp.float32,
    )
    flat = jnp.concatenate([gram[:half, rank:], gram[half:rank, rank:]], axis=1)
    for side in range(CORES):
        l_part[side] = flat[side * half_rows:(side + 1) * half_rows, :]

    to_partner = remote(l_part.at[1 - core], l_recv, ps_sem, pr_sem, partner)
    to_partner.start()
    to_partner.wait_recv()
    l_half[...] = l_part[core] + l_recv[...]

    def spread_half(mask):
        target = flip(chip, mask) * CORES + core
        return remote(l_half, h_recv.at[mask - 1], hs_sem, hr_sem, target)

    for mask in range(chips - 1, 0, -1):
        spread_half(mask).start()
    for piece in pieces:
        to_core(piece).wait_send()
    for mask in range(1, chips):
        to_chip(mask).wait_send()
    to_partner.wait_send()
    for copy in copy_q:
        copy.wait()
    pltpu.make_async_copy(h_recv, h_recv, hr_sem).wait()
    whole = l_half[...]
    for mask in range(1, chips):
        whole = whole + h_recv[mask - 1]
    l_all[core] = whole
    share_half = remote(l_all.at[core], l_all.at[core], as_sem, ar_sem, partner)
    share_half.start()

    def products(side, start):
        acc = start
        for r in range(half_rows):
            acc = acc + q_buf[side, :, r * LANES:(r + 1) * LANES].astype(jnp.float32) * l_all[side, r:r + 1, :]
        return acc

    acc = products(core, jnp.zeros((queries.shape[0], LANES), jnp.float32))
    remote(l_all.at[1 - core], l_all.at[1 - core], as_sem, ar_sem, partner).wait_recv()
    acc = products(1 - core, acc)
    dots = jnp.sum(acc, axis=1, keepdims=True)
    row = lax.broadcasted_iota(jnp.int32, acc.shape, 0)
    lane = lax.broadcasted_iota(jnp.int32, acc.shape, 1)
    across = jnp.sum(jnp.where(row == lane, dots, 0.0), axis=0, keepdims=True)
    rows = result.shape[0] - 1
    result[rows:, :] = across
    if rows < CORES * half_rows:
        first = me * rows
        result[:rows, :] = l_all[first // half_rows, pl.ds(lax.rem(first, half_rows), rows), :]
    else:
        for side in range(CORES):
            result[side * half_rows:(side + 1) * half_rows, :] = l_all[side]
    share_half.wait_send()
    pltpu.make_async_copy(h_recv, h_recv, hs_sem).wait()


def on_device(hidden, grad, in_factor, out_factor, queries):
    n = lax.axis_size("dp")
    tokens, width_h = hidden.shape
    width_g = grad.shape[1]
    rank = in_factor.shape[1]
    count_q, features = queries.shape
    chips = n // CORES
    block = tokens // n
    chunk = tokens // (2 * CHUNKS)
    flat_rows = features // LANES
    half_rows = flat_rows // CORES
    share = features // n
    rows = share // LANES if share % LANES == 0 else flat_rows
    f32, b16 = jnp.float32, jnp.bfloat16
    dma = pltpu.SemaphoreType.DMA
    result = pl.pallas_call(
        functools.partial(kernel, n),
        out_shape=jax.ShapeDtypeStruct((rows + 1, LANES), f32),
        in_specs=[pl.BlockSpec(memory_space=pl.ANY)] * 5,
        out_specs=pl.BlockSpec(memory_space=pltpu.VMEM),
        scratch_shapes=[
            pltpu.VMEM((2 * CHUNKS, chunk, width_h), b16),
            pltpu.VMEM((2 * CHUNKS, chunk, width_g), b16),
            pltpu.VMEM((rank, width_h), b16),
            pltpu.VMEM((rank, width_g), b16),
            pltpu.VMEM((CORES, count_q, features // CORES), b16),
            pltpu.VMEM((width_h, 2 * rank), b16),
            pltpu.VMEM((width_g, 2 * rank), b16),
            pltpu.VMEM((tokens // 2, 2 * rank), f32),
            pltpu.VMEM((tokens // 2, 2 * rank), f32),
            pltpu.VMEM((tokens // 2, 2 * rank), f32),
            pltpu.VMEM((chips - 1, block, 2 * rank), b16),
            pltpu.VMEM((chips - 1, block, 2 * rank), b16),
            pltpu.VMEM((CORES, half_rows, LANES), f32),
            pltpu.VMEM((half_rows, LANES), f32),
            pltpu.VMEM((half_rows, LANES), f32),
            pltpu.VMEM((chips - 1, half_rows, LANES), f32),
            pltpu.VMEM((CORES, half_rows, LANES), f32),
            dma((4 * CHUNKS + 2 + CORES,)),
            dma((chips // PAIR,)),
            dma((chips // PAIR,)),
            dma((chips - 1,)),
            dma((chips - 1,)),
            dma, dma, dma, dma, dma, dma,
        ],
        compiler_params=pltpu.CompilerParams(
            collective_id=0, has_side_effects=True, vmem_limit_bytes=VMEM_BYTES
        ),
        cost_estimate=pl.CostEstimate(
            flops=4 * rank * tokens * (width_h + width_g),
            bytes_accessed=2 * tokens * (width_h + width_g),
            transcendentals=0,
        ),
    )(hidden, grad, in_factor.T, out_factor.T, queries)
    logged = result[:rows].reshape(1, rows * LANES)
    if rows == flat_rows:
        logged = lax.dynamic_slice_in_dim(logged, lax.axis_index("dp") * share, share, 1)
    return logged, result[rows:, :count_q]


def solution(mesh):
    in_specs = (P("groups", "dp"), P("groups", "dp"), P("dp", None), P("dp", None), P("dp", None))
    out_specs = (P("groups", "dp"), P("groups", "dp"))
    return jax.shard_map(
        on_device, mesh=mesh, in_specs=in_specs, out_specs=out_specs, check_vma=False
    )
```

```python
import functools

import jax
import jax.numpy as jnp
from jax import lax
from jax.experimental import pallas as pl
from jax.experimental.pallas import tpu as pltpu
from jax.sharding import PartitionSpec as P

CORES = 2
PIECES = 4
MEET = 2
LANES = 128
VMEM_BYTES = 56 * 2**20


def flip(value, mask):
    bit = 1
    while bit <= mask:
        if mask & bit:
            value = value + bit - 2 * bit * lax.rem(value // bit, 2)
        bit *= 2
    return value


def kernel(
    n,
    hidden, grad, a_in, b_in, queries,
    result,
    hbuf, gbuf, a_buf, b_buf, q_buf, wa, wb,
    part_send, part_recv, own, z_send, z_recv,
    l_part, l_recv, l_half, h_recv, l_all,
    in_sem, cs_sem, cr_sem, zs_sem, zr_sem,
    ps_sem, pr_sem, hs_sem, hr_sem, as_sem, ar_sem,
):
    me = lax.axis_index("dp")
    core = lax.rem(me, CORES)
    chip = me // CORES
    chips = n // CORES
    chunk = hbuf.shape[1]
    pieces = own.shape[0]
    group = chips // pieces
    block = chunk // group
    rank = a_in.shape[0]
    half_rows = l_half.shape[0]
    partner = chip * CORES + 1 - core

    def remote(src, dst, send, recv, target):
        return pltpu.make_async_remote_copy(
            src_ref=src, dst_ref=dst, send_sem=send, recv_sem=recv,
            device_id={"dp": target}, device_id_type=pl.DeviceIdType.MESH,
        )

    barrier = pltpu.get_barrier_semaphore()

    def greet(target):
        pl.semaphore_signal(
            barrier, inc=1, device_id={"dp": target}, device_id_type=pl.DeviceIdType.MESH
        )

    for mask in range(chips - 1, 0, -1):
        greet(flip(chip, mask) * CORES + core)
    greet(partner)

    def inputs(mine, piece):
        first = ((core if mine else 1 - core) * pieces + flip(chip // group, piece)) * chunk
        span = pl.ds(pl.multiple_of(first, chunk), chunk)
        slot = mine * pieces + piece
        return (
            pltpu.make_async_copy(hidden.at[span], hbuf.at[slot], in_sem.at[2 * slot]),
            pltpu.make_async_copy(grad.at[span], gbuf.at[slot], in_sem.at[2 * slot + 1]),
        )

    last = 4 * pieces
    copy_a = pltpu.make_async_copy(a_in, a_buf, in_sem.at[last])
    copy_b = pltpu.make_async_copy(b_in, b_buf, in_sem.at[last + 1])
    width_q = q_buf.shape[2]
    copy_q = [
        pltpu.make_async_copy(
            queries.at[:, pl.ds(side * width_q, width_q)], q_buf.at[side], in_sem.at[last + 2 + side]
        )
        for side in range(CORES)
    ]
    copy_a.start()
    copy_b.start()
    far = list(range(pieces - 1, -1, -1))
    order = [(0, far[0]), (0, far[1])]
    for place in range(2, pieces):
        order += [(1, far[place - 2]), (0, far[place])]
    order += [(1, far[-2]), (1, far[-1])]
    for mine, step in order:
        for copy in inputs(mine, step):
            copy.start()
    for copy in copy_q:
        copy.start()

    row = lax.broadcasted_iota(jnp.int32, (rank, 2 * rank), 0)
    lane = lax.broadcasted_iota(jnp.int32, (rank, 2 * rank), 1)
    half = rank // 2
    source = jnp.where(lane < half, 2 * lane, 2 * (lane - half) + 1)
    take_a = jnp.where((lane < rank) & (row == source), 1.0, 0.0).astype(jnp.bfloat16)
    take_b = jnp.where(lane - rank == row, 1.0, 0.0).astype(jnp.bfloat16)

    def spread(factor, take):
        return lax.dot_general(
            factor[...], take, (((0,), (0,)), ((), ())), preferred_element_type=jnp.float32
        ).astype(jnp.bfloat16)

    copy_a.wait()
    wa[...] = spread(a_buf, take_a)
    copy_b.wait()
    wb[...] = spread(b_buf, take_b)

    def project(mine, piece):
        for copy in inputs(mine, piece):
            copy.wait()
        slot = mine * pieces + piece
        (own if mine else part_send)[piece] = jnp.dot(
            hbuf[slot], wa[...], preferred_element_type=jnp.float32
        ) + jnp.dot(gbuf[slot], wb[...], preferred_element_type=jnp.float32)

    def to_core(piece):
        return remote(part_send.at[piece], part_recv.at[piece], cs_sem.at[piece], cr_sem.at[piece], partner)

    def to_chip(mask):
        slot = mask - 1
        target = flip(chip, mask) * CORES + core
        return remote(z_send.at[slot], z_recv.at[slot], zs_sem.at[slot], zr_sem.at[slot], target)

    def chip_sum(mask):
        place = lax.rem(flip(chip, mask), group)
        span = pl.ds(pl.multiple_of(place * block, block), block)
        return own[mask // group, span, :] + part_recv[mask // group, span, :]

    def send_chips(piece):
        to_core(piece).wait_recv()
        for mask in range((piece + 1) * group - 1, piece * group - 1, -1):
            if mask:
                z_send[mask - 1] = chip_sum(mask).astype(jnp.bfloat16)
                to_chip(mask).start()

    waiting, open_pieces = [], []
    for place, (mine, piece) in enumerate(order):
        project(mine, piece)
        if open_pieces and place >= MEET:
            send_chips(open_pieces.pop(0))
        (open_pieces if mine else waiting).append(piece)
        if place == MEET - 1:
            pl.semaphore_wait(barrier, chips)
        if place >= MEET - 1:
            for sending in waiting:
                to_core(sending).start()
            waiting = []
    for piece in open_pieces:
        send_chips(piece)
    value = chip_sum(0)
    for mask in range(chips - 1, 0, -1):
        to_chip(mask).wait_recv()
        value = value + z_recv[mask - 1].astype(jnp.float32)

    gram = lax.dot_general(
        value, value, (((0,), (0,)), ((), ())),
        precision=lax.Precision.HIGHEST, preferred_element_type=jnp.float32,
    )
    flat = jnp.concatenate([gram[:half, rank:], gram[half:rank, rank:]], axis=1)
    for side in range(CORES):
        l_part[side] = flat[side * half_rows:(side + 1) * half_rows, :]

    to_partner = remote(l_part.at[1 - core], l_recv, ps_sem, pr_sem, partner)
    to_partner.start()
    to_partner.wait_recv()
    l_half[...] = l_part[core] + l_recv[...]

    def spread_half(mask):
        target = flip(chip, mask) * CORES + core
        return remote(l_half, h_recv.at[mask - 1], hs_sem, hr_sem, target)

    for mask in range(chips - 1, 0, -1):
        spread_half(mask).start()
    for piece in far:
        to_core(piece).wait_send()
    for mask in range(1, chips):
        to_chip(mask).wait_send()
    to_partner.wait_send()
    for copy in copy_q:
        copy.wait()
    pltpu.make_async_copy(h_recv, h_recv, hr_sem).wait()
    whole = l_half[...]
    for mask in range(1, chips):
        whole = whole + h_recv[mask - 1]
    l_all[core] = whole
    share_half = remote(l_all.at[core], l_all.at[core], as_sem, ar_sem, partner)
    share_half.start()

    def products(side, start):
        acc = start
        for r in range(half_rows):
            acc = acc + q_buf[side, :, r * LANES:(r + 1) * LANES].astype(jnp.float32) * l_all[side, r:r + 1, :]
        return acc

    acc = products(core, jnp.zeros((queries.shape[0], LANES), jnp.float32))
    remote(l_all.at[1 - core], l_all.at[1 - core], as_sem, ar_sem, partner).wait_recv()
    acc = products(1 - core, acc)
    dots = jnp.sum(acc, axis=1, keepdims=True)
    row = lax.broadcasted_iota(jnp.int32, acc.shape, 0)
    lane = lax.broadcasted_iota(jnp.int32, acc.shape, 1)
    across = jnp.sum(jnp.where(row == lane, dots, 0.0), axis=0, keepdims=True)
    rows = result.shape[0] - 1
    result[rows:, :] = across
    if rows < CORES * half_rows:
        first = me * rows
        result[:rows, :] = l_all[first // half_rows, pl.ds(lax.rem(first, half_rows), rows), :]
    else:
        for side in range(CORES):
            result[side * half_rows:(side + 1) * half_rows, :] = l_all[side]
    share_half.wait_send()
    pltpu.make_async_copy(h_recv, h_recv, hs_sem).wait()


def split(rows, result, logged, scores):
    logged[...] = result[:rows, :]
    scores[...] = result[rows:, :scores.shape[1]]


def on_device(hidden, grad, in_factor, out_factor, queries):
    n = lax.axis_size("dp")
    tokens, width_h = hidden.shape
    width_g = grad.shape[1]
    rank = in_factor.shape[1]
    count_q, features = queries.shape
    chips = n // CORES
    block = tokens // n
    pieces = min(PIECES, chips)
    chunk = tokens // (2 * pieces)
    flat_rows = features // LANES
    half_rows = flat_rows // CORES
    share = features // n
    rows = share // LANES if share % LANES == 0 else flat_rows
    f32, b16 = jnp.float32, jnp.bfloat16
    dma = pltpu.SemaphoreType.DMA
    result = pl.pallas_call(
        functools.partial(kernel, n),
        out_shape=jax.ShapeDtypeStruct((rows + 1, LANES), f32),
        in_specs=[pl.BlockSpec(memory_space=pl.ANY)] * 5,
        out_specs=pl.BlockSpec(memory_space=pltpu.VMEM),
        scratch_shapes=[
            pltpu.VMEM((2 * pieces, chunk, width_h), b16),
            pltpu.VMEM((2 * pieces, chunk, width_g), b16),
            pltpu.VMEM((rank, width_h), b16),
            pltpu.VMEM((rank, width_g), b16),
            pltpu.VMEM((CORES, count_q, features // CORES), b16),
            pltpu.VMEM((width_h, 2 * rank), b16),
            pltpu.VMEM((width_g, 2 * rank), b16),
            pltpu.VMEM((pieces, chunk, 2 * rank), f32),
            pltpu.VMEM((pieces, chunk, 2 * rank), f32),
            pltpu.VMEM((pieces, chunk, 2 * rank), f32),
            pltpu.VMEM((chips - 1, block, 2 * rank), b16),
            pltpu.VMEM((chips - 1, block, 2 * rank), b16),
            pltpu.VMEM((CORES, half_rows, LANES), f32),
            pltpu.VMEM((half_rows, LANES), f32),
            pltpu.VMEM((half_rows, LANES), f32),
            pltpu.VMEM((chips - 1, half_rows, LANES), f32),
            pltpu.VMEM((CORES, half_rows, LANES), f32),
            dma((4 * pieces + 2 + CORES,)),
            dma((pieces,)),
            dma((pieces,)),
            dma((chips - 1,)),
            dma((chips - 1,)),
            dma, dma, dma, dma, dma, dma,
        ],
        compiler_params=pltpu.CompilerParams(
            collective_id=0, has_side_effects=True, vmem_limit_bytes=VMEM_BYTES
        ),
        cost_estimate=pl.CostEstimate(
            flops=4 * rank * tokens * (width_h + width_g),
            bytes_accessed=2 * tokens * (width_h + width_g),
            transcendentals=0,
        ),
    )(hidden, grad, in_factor.T, out_factor.T, queries)
    if rows < flat_rows:
        logged, scores = pl.pallas_call(
            functools.partial(split, rows),
            out_shape=(
                jax.ShapeDtypeStruct((rows, LANES), f32),
                jax.ShapeDtypeStruct((1, count_q), f32),
            ),
            in_specs=[pl.BlockSpec(memory_space=pltpu.VMEM)],
            out_specs=(pl.BlockSpec(memory_space=pltpu.VMEM),) * 2,
        )(result)
        return logged.reshape(1, share), scores
    logged = result[:rows].reshape(1, rows * LANES)
    if rows == flat_rows:
        logged = lax.dynamic_slice_in_dim(logged, lax.axis_index("dp") * share, share, 1)
    return logged, result[rows:, :count_q]


def solution(mesh):
    in_specs = (P("groups", "dp"), P("groups", "dp"), P("dp", None), P("dp", None), P("dp", None))
    out_specs = (P("groups", "dp"), P("groups", "dp"))
    return jax.shard_map(
        on_device, mesh=mesh, in_specs=in_specs, out_specs=out_specs, check_vma=False
    )
```

```python
import functools

import jax
import jax.numpy as jnp
from jax import lax
from jax.experimental import pallas as pl
from jax.experimental.pallas import tpu as pltpu
from jax.sharding import PartitionSpec as P

CORES = 2
PIECES = 4
MEET = 2
LANES = 128
VMEM_BYTES = 56 * 2**20


def flip(value, mask):
    bit = 1
    while bit <= mask:
        if mask & bit:
            value = value + bit - 2 * bit * lax.rem(value // bit, 2)
        bit *= 2
    return value


def kernel(
    n,
    hidden, grad, a_in, b_in, queries,
    result,
    hbuf, gbuf, a_buf, b_buf, q_buf, wa, wb,
    part_send, part_recv, own, z_send, z_recv,
    l_part, l_recv, l_half, h_recv, l_all,
    in_sem, cs_sem, cr_sem, zs_sem, zr_sem,
    ps_sem, pr_sem, hs_sem, hr_sem,
):
    me = lax.axis_index("dp")
    core = lax.rem(me, CORES)
    chip = me // CORES
    chips = n // CORES
    chunk = hbuf.shape[1]
    pieces = own.shape[0]
    group = chips // pieces
    block = chunk // group
    rank = a_in.shape[0]
    half_rows = l_half.shape[1]
    partner = chip * CORES + 1 - core

    def remote(src, dst, send, recv, target):
        return pltpu.make_async_remote_copy(
            src_ref=src, dst_ref=dst, send_sem=send, recv_sem=recv,
            device_id={"dp": target}, device_id_type=pl.DeviceIdType.MESH,
        )

    barrier = pltpu.get_barrier_semaphore()

    def greet(target):
        pl.semaphore_signal(
            barrier, inc=1, device_id={"dp": target}, device_id_type=pl.DeviceIdType.MESH
        )

    for mask in range(chips - 1, 0, -1):
        greet(flip(chip, mask) * CORES + core)
    greet(partner)

    def inputs(mine, piece):
        first = ((core if mine else 1 - core) * pieces + flip(chip // group, piece)) * chunk
        span = pl.ds(pl.multiple_of(first, chunk), chunk)
        slot = mine * pieces + piece
        return (
            pltpu.make_async_copy(hidden.at[span], hbuf.at[slot], in_sem.at[2 * slot]),
            pltpu.make_async_copy(grad.at[span], gbuf.at[slot], in_sem.at[2 * slot + 1]),
        )

    last = 4 * pieces
    copy_a = pltpu.make_async_copy(a_in, a_buf, in_sem.at[last])
    copy_b = pltpu.make_async_copy(b_in, b_buf, in_sem.at[last + 1])
    width_q = q_buf.shape[2]
    copy_q = [
        pltpu.make_async_copy(
            queries.at[:, pl.ds(side * width_q, width_q)], q_buf.at[side], in_sem.at[last + 2 + side]
        )
        for side in range(CORES)
    ]
    copy_a.start()
    copy_b.start()
    far = list(range(pieces - 1, -1, -1))
    order = [(0, far[0]), (0, far[1])]
    for place in range(2, pieces):
        order += [(1, far[place - 2]), (0, far[place])]
    order += [(1, far[-2]), (1, far[-1])]
    for mine, step in order:
        for copy in inputs(mine, step):
            copy.start()
    for copy in copy_q:
        copy.start()

    row = lax.broadcasted_iota(jnp.int32, (rank, 2 * rank), 0)
    lane = lax.broadcasted_iota(jnp.int32, (rank, 2 * rank), 1)
    half = rank // 2
    source = jnp.where(lane < half, 2 * lane, 2 * (lane - half) + 1)
    take_a = jnp.where((lane < rank) & (row == source), 1.0, 0.0).astype(jnp.bfloat16)
    take_b = jnp.where(lane - rank == row, 1.0, 0.0).astype(jnp.bfloat16)

    def spread(factor, take):
        return lax.dot_general(
            factor[...], take, (((0,), (0,)), ((), ())), preferred_element_type=jnp.float32
        ).astype(jnp.bfloat16)

    copy_a.wait()
    wa[...] = spread(a_buf, take_a)
    copy_b.wait()
    wb[...] = spread(b_buf, take_b)

    def project(mine, piece):
        for copy in inputs(mine, piece):
            copy.wait()
        slot = mine * pieces + piece
        (own if mine else part_send)[piece] = jnp.dot(
            hbuf[slot], wa[...], preferred_element_type=jnp.float32
        ) + jnp.dot(gbuf[slot], wb[...], preferred_element_type=jnp.float32)

    def to_core(piece):
        return remote(part_send.at[piece], part_recv.at[piece], cs_sem.at[piece], cr_sem.at[piece], partner)

    def to_chip(mask):
        slot = mask - 1
        target = flip(chip, mask) * CORES + core
        return remote(z_send.at[slot], z_recv.at[slot], zs_sem.at[slot], zr_sem.at[slot], target)

    def chip_sum(mask):
        place = lax.rem(flip(chip, mask), group)
        span = pl.ds(pl.multiple_of(place * block, block), block)
        return own[mask // group, span, :] + part_recv[mask // group, span, :]

    def send_chips(piece):
        to_core(piece).wait_recv()
        for mask in range((piece + 1) * group - 1, piece * group - 1, -1):
            if mask:
                z_send[mask - 1] = chip_sum(mask).astype(jnp.bfloat16)
                to_chip(mask).start()

    waiting, open_pieces = [], []
    for place, (mine, piece) in enumerate(order):
        project(mine, piece)
        if open_pieces and place >= MEET:
            send_chips(open_pieces.pop(0))
        (open_pieces if mine else waiting).append(piece)
        if place == MEET - 1:
            pl.semaphore_wait(barrier, chips)
        if place >= MEET - 1:
            for sending in waiting:
                to_core(sending).start()
            waiting = []
    for piece in open_pieces:
        send_chips(piece)
    value = chip_sum(0)
    for mask in range(chips - 1, 0, -1):
        to_chip(mask).wait_recv()
        value = value + z_recv[mask - 1].astype(jnp.float32)

    gram = lax.dot_general(
        value, value, (((0,), (0,)), ((), ())),
        precision=lax.Precision.HIGHEST, preferred_element_type=jnp.float32,
    )
    flat = jnp.concatenate([gram[:half, rank:], gram[half:rank, rank:]], axis=1)
    for side in range(CORES):
        l_part[side] = flat[side * half_rows:(side + 1) * half_rows, :]

    l_half[...] = l_part[...]

    def spread_half(mask):
        target = flip(chip, mask) * CORES + core
        return remote(l_half, h_recv.at[mask - 1], hs_sem, hr_sem, target)

    for mask in range(chips - 1, 0, -1):
        spread_half(mask).start()
    for piece in far:
        to_core(piece).wait_send()
    for mask in range(1, chips):
        to_chip(mask).wait_send()
    for copy in copy_q:
        copy.wait()
    pltpu.make_async_copy(h_recv, h_recv, hr_sem).wait()
    whole = l_half[...]
    for mask in range(1, chips):
        whole = whole + h_recv[mask - 1]
    l_part[...] = whole
    to_partner = remote(l_part, l_recv, ps_sem, pr_sem, partner)
    to_partner.start()
    to_partner.wait_recv()
    l_all[...] = whole + l_recv[...]

    def products(side, start):
        acc = start
        for r in range(half_rows):
            acc = acc + q_buf[side, :, r * LANES:(r + 1) * LANES].astype(jnp.float32) * l_all[side, r:r + 1, :]
        return acc

    acc = products(core, jnp.zeros((queries.shape[0], LANES), jnp.float32))
    acc = products(1 - core, acc)
    dots = jnp.sum(acc, axis=1, keepdims=True)
    row = lax.broadcasted_iota(jnp.int32, acc.shape, 0)
    lane = lax.broadcasted_iota(jnp.int32, acc.shape, 1)
    across = jnp.sum(jnp.where(row == lane, dots, 0.0), axis=0, keepdims=True)
    rows = result.shape[0] - 1
    result[rows:, :] = across
    if rows < CORES * half_rows:
        first = me * rows
        result[:rows, :] = l_all[first // half_rows, pl.ds(lax.rem(first, half_rows), rows), :]
    else:
        for side in range(CORES):
            result[side * half_rows:(side + 1) * half_rows, :] = l_all[side]
    to_partner.wait_send()
    pltpu.make_async_copy(h_recv, h_recv, hs_sem).wait()


def split(rows, result, logged, scores):
    logged[...] = result[:rows, :]
    scores[...] = result[rows:, :scores.shape[1]]


def on_device(hidden, grad, in_factor, out_factor, queries):
    n = lax.axis_size("dp")
    tokens, width_h = hidden.shape
    width_g = grad.shape[1]
    rank = in_factor.shape[1]
    count_q, features = queries.shape
    chips = n // CORES
    block = tokens // n
    pieces = min(PIECES, chips)
    chunk = tokens // (2 * pieces)
    flat_rows = features // LANES
    half_rows = flat_rows // CORES
    share = features // n
    rows = share // LANES if share % LANES == 0 else flat_rows
    f32, b16 = jnp.float32, jnp.bfloat16
    dma = pltpu.SemaphoreType.DMA
    result = pl.pallas_call(
        functools.partial(kernel, n),
        out_shape=jax.ShapeDtypeStruct((rows + 1, LANES), f32),
        in_specs=[pl.BlockSpec(memory_space=pl.ANY)] * 5,
        out_specs=pl.BlockSpec(memory_space=pltpu.VMEM),
        scratch_shapes=[
            pltpu.VMEM((2 * pieces, chunk, width_h), b16),
            pltpu.VMEM((2 * pieces, chunk, width_g), b16),
            pltpu.VMEM((rank, width_h), b16),
            pltpu.VMEM((rank, width_g), b16),
            pltpu.VMEM((CORES, count_q, features // CORES), b16),
            pltpu.VMEM((width_h, 2 * rank), b16),
            pltpu.VMEM((width_g, 2 * rank), b16),
            pltpu.VMEM((pieces, chunk, 2 * rank), f32),
            pltpu.VMEM((pieces, chunk, 2 * rank), f32),
            pltpu.VMEM((pieces, chunk, 2 * rank), f32),
            pltpu.VMEM((chips - 1, block, 2 * rank), b16),
            pltpu.VMEM((chips - 1, block, 2 * rank), b16),
            pltpu.VMEM((CORES, half_rows, LANES), f32),
            pltpu.VMEM((CORES, half_rows, LANES), f32),
            pltpu.VMEM((CORES, half_rows, LANES), f32),
            pltpu.VMEM((chips - 1, CORES, half_rows, LANES), f32),
            pltpu.VMEM((CORES, half_rows, LANES), f32),
            dma((4 * pieces + 2 + CORES,)),
            dma((pieces,)),
            dma((pieces,)),
            dma((chips - 1,)),
            dma((chips - 1,)),
            dma, dma, dma, dma,
        ],
        compiler_params=pltpu.CompilerParams(
            collective_id=0, has_side_effects=True, vmem_limit_bytes=VMEM_BYTES
        ),
        cost_estimate=pl.CostEstimate(
            flops=4 * rank * tokens * (width_h + width_g),
            bytes_accessed=2 * tokens * (width_h + width_g),
            transcendentals=0,
        ),
    )(hidden, grad, in_factor.T, out_factor.T, queries)
    if rows < flat_rows:
        logged, scores = pl.pallas_call(
            functools.partial(split, rows),
            out_shape=(
                jax.ShapeDtypeStruct((rows, LANES), f32),
                jax.ShapeDtypeStruct((1, count_q), f32),
            ),
            in_specs=[pl.BlockSpec(memory_space=pltpu.VMEM)],
            out_specs=(pl.BlockSpec(memory_space=pltpu.VMEM),) * 2,
        )(result)
        return logged.reshape(1, share), scores
    logged = result[:rows].reshape(1, rows * LANES)
    if rows == flat_rows:
        logged = lax.dynamic_slice_in_dim(logged, lax.axis_index("dp") * share, share, 1)
    return logged, result[rows:, :count_q]


def solution(mesh):
    in_specs = (P("groups", "dp"), P("groups", "dp"), P("dp", None), P("dp", None), P("dp", None))
    out_specs = (P("groups", "dp"), P("groups", "dp"))
    return jax.shard_map(
        on_device, mesh=mesh, in_specs=in_specs, out_specs=out_specs, check_vma=False
    )
```
